512 devices in a mesh: depth: 2 (over x_hi), row: 16 (over x_lo, y), col: 16 (over z, core).
Axes of the slice: x: 4 (x_hi: 2, x_lo: 2; x = x_hi * 2 + x_lo), y: 8, z: 8, core: 2. Of those that a mesh axis runs over, the one named last changes fastest.
Arguments:
- tokens: bfloat16 [768, 8192], P(('depth', 'row'), 'col'), may hold values from -6 to 6
- gate_weight: bfloat16 [8192, 14336], P('col', 'row'), may hold values from -0.0625 to 0.0625
- up_weight: bfloat16 [8192, 14336], P('col', 'row'), may hold values from -0.0625 to 0.0625
- down_weight: bfloat16 [14336, 8192], P('row', 'col'), may hold values from -0.046875 to 0.046875
Outputs:
- mixed: bfloat16 [768, 8192], P(('depth', 'row'), 'col')
The draws below stay inside these ranges and needn't reach their ends.
All inputs are finite; a program needn't handle non-finite values.
Results may differ from the reference program's by a relative error of at most 0.0049.
Values may be sent and summed in bfloat16 or wider, within the bound.
A program may use at most 64 MiB of HBM per device.

```python
import jax
import jax.numpy as jnp

D = 8192
FF = 14336
TOKENS = 768


def block_scale(own_key, shape, pieces, smallest, high):
    def one(position, blocks):
        heights = jax.random.uniform(jax.random.fold_in(jax.random.fold_in(own_key, 6), position), (blocks,), jnp.float32, smallest / len(pieces), high / len(pieces))
        return jnp.repeat(jnp.exp(heights), shape[position] // blocks).reshape((-1,) + (1,) * (len(shape) - position - 1))

    level = one(*pieces[0])
    for cut in pieces[1:]:
        level = level * one(*cut)
    return level


def scatter_about(stream_key, shape, deviation, limit, split=(), kind=jnp.bfloat16):
    values = deviation * jax.random.normal(stream_key, shape, jnp.float32)
    if split:
        values = values * block_scale(stream_key, shape, split, -0.22, 0.18)
    return jnp.clip(values, -limit, limit).astype(kind)


def setup_inputs(seed: int = 0) -> dict:
    streams_of = jax.random.split(jax.random.key(seed), 5)
    tokens = scatter_about(streams_of[0], (TOKENS, D), 1.0, 6.0, ((0, 32), (1, 16)))
    gate_weight = scatter_about(streams_of[1], (D, FF), D ** -0.5, 0.0625, ((0, 16), (1, 16)))
    up_weight = scatter_about(streams_of[2], (D, FF), D ** -0.5, 0.0625, ((0, 16), (1, 16)))
    down_weight = scatter_about(streams_of[3], (FF, D), FF ** -0.5, 0.046875, ((0, 16), (1, 16)))
    return dict(tokens=tokens, gate_weight=gate_weight, up_weight=up_weight, down_weight=down_weight)


def reference(tokens, gate_weight, up_weight, down_weight):
    gate = jnp.dot(tokens, gate_weight, preferred_element_type=jnp.float32)
    up = jnp.dot(tokens, up_weight, preferred_element_type=jnp.float32)
    hidden = (jax.nn.silu(gate) * up).astype(jnp.bfloat16)
    mixed = jnp.dot(hidden, down_weight, preferred_element_type=jnp.float32)
    return mixed.astype(jnp.bfloat16)
```

```python
import functools

import jax
import jax.numpy as jnp
from jax import lax
from jax.experimental import pallas as pl
from jax.experimental.pallas import tpu as pltpu
from jax.sharding import PartitionSpec as P

MESH = pl.DeviceIdType.MESH
NX, NY, NZ, NC = 2, 8, 8, 2
CHUNKS = ((0, 512), (512, 384))
F32, BF16 = jnp.float32, jnp.bfloat16


def kernel(
    tok, gate, up, down, out,
    wg, wu, wd, tok_all, gate_sum, up_sum, send_b0, send_b1, recv_b0, recv_b1, hid0, hid1, part, send_c, recv_c,
    load_sem, wss, wrs, ass, ars, bss, brs, hss, hrs, css, crs,
):
    depth, row, col = lax.axis_index("depth"), lax.axis_index("row"), lax.axis_index("col")
    x, y = row // NY, lax.rem(row, NY)
    z, core = col // NC, lax.rem(col, NC)
    rows, kd = tok.shape
    home = x == core

    def at(xx, yy, zz, cc):
        return (depth, xx * NY + yy, zz * NC + cc)

    def around(v, n, by):
        return lax.rem(v + by, n)

    def remote(src, dst, ss, rs, device):
        return pltpu.make_async_remote_copy(src, dst, ss, rs, device_id=device, device_id_type=MESH)

    mine = pl.ds(pl.multiple_of(core * kd, kd), kd)
    loads = [
        pltpu.make_async_copy(gate, wg.at[mine], load_sem.at[0]),
        pltpu.make_async_copy(up, wu.at[mine], load_sem.at[1]),
        pltpu.make_async_copy(down, wd.at[core], load_sem.at[2]),
    ]
    for copy in loads:
        copy.start()

    barrier = pltpu.get_barrier_semaphore()

    def greet(device):
        pl.semaphore_signal(barrier, inc=1, device_id=device, device_id_type=MESH)

    def greet_row(i, c):
        dx, dy = i // NY, lax.rem(i, NY)
        for device in (
            at(around(x, NX, dx), around(y, NY, dy), z, x),
            at(core, around(y, NY, dy), z, around(core, NC, dx)),
        ):
            @pl.when(jnp.logical_not(jnp.logical_and(home, i == 0)))
            def _():
                greet(device)

        return c

    lax.fori_loop(0, NX * NY, greet_row, 0)

    def greet_col(i, c):
        greet(at(x, y, around(z, NZ, i), core))
        return c

    lax.fori_loop(1, NZ, greet_col, 0)
    greet(at(x, y, z, 1 - core))
    pl.semaphore_wait(barrier, 2 * NX * NY + NZ - jnp.where(home, 2, 0))

    def tok_copy(i):
        dx, dy = i // NY, lax.rem(i, NY)
        return remote(
            tok, tok_all.at[y, core], ass.at[i], ars.at[y, core], at(around(x, NX, dx), around(y, NY, dy), z, x)
        )

    def tok_send(i, c):
        own = jnp.logical_and(home, i == 0)

        @pl.when(own)
        def _():
            pltpu.make_async_copy(tok, tok_all.at[y, core], ars.at[y, core]).start()

        @pl.when(jnp.logical_not(own))
        def _():
            tok_copy(i).start()

        return c

    lax.fori_loop(0, NX * NY, tok_send, 0)

    other = at(x, y, z, 1 - core)
    swaps = [
        remote(gate, wg.at[mine], wss.at[0], wrs.at[0], other),
        remote(up, wu.at[mine], wss.at[1], wrs.at[1], other),
        remote(down, wd.at[core], wss.at[2], wrs.at[2], other),
    ]
    for copy in swaps:
        copy.start()

    def tok_wait(i, c):
        yy, cc = i // NC, lax.rem(i, NC)
        pltpu.make_async_copy(tok, tok_all.at[yy, cc], ars.at[yy, cc]).wait()
        return c

    lax.fori_loop(0, NY * NC, tok_wait, 0)
    loads[0].wait()
    swaps[0].wait_recv()
    loads[1].wait()
    swaps[1].wait_recv()

    lhs = jnp.concatenate(
        [tok_all[:, cc].astype(F32).reshape(NY * rows, kd).astype(BF16) for cc in range(NC)], axis=1
    )

    send_b, recv_b, hid = (send_b0, send_b1), (recv_b0, recv_b1), (hid0, hid1)

    def sum_copy(ch, i):
        return remote(
            send_b[ch].at[i - 1], recv_b[ch].at[i - 1], bss.at[ch, i - 1], brs.at[ch, i - 1],
            at(x, y, around(z, NZ, i), core),
        )

    def hid_copy(ch, i):
        return remote(
            hid[ch].at[z], hid[ch].at[z], hss.at[ch, i - 1], hrs.at[ch, i - 1], at(x, y, around(z, NZ, i), core)
        )

    def own_rows(zz):
        return pl.ds(pl.multiple_of(zz * rows, 8), rows)

    for ch, (lo, width) in enumerate(CHUNKS):
        cols = pl.ds(lo, width)
        gate_sum[:, cols] = jnp.dot(lhs, wg[:, cols], preferred_element_type=F32)
        up_sum[:, cols] = jnp.dot(lhs, wu[:, cols], preferred_element_type=F32)

        def sum_send(i, c):
            there = own_rows(around(z, NZ, i))
            both = jnp.concatenate([gate_sum[there, cols], up_sum[there, cols]], axis=0)
            send_b[ch][i - 1] = both.astype(BF16)
            sum_copy(ch, i).start()
            return c

        lax.fori_loop(1, NZ, sum_send, 0)

    for ch, (lo, width) in enumerate(CHUNKS):
        cols = pl.ds(lo, width)
        both = jnp.concatenate([gate_sum[own_rows(z), cols], up_sum[own_rows(z), cols]], axis=0)
        for i in range(1, NZ):
            sum_copy(ch, i).wait_recv()
            both = both + recv_b[ch][i - 1].astype(F32)
        hid[ch][z] = (jax.nn.silu(both[:rows]) * both[rows:]).astype(BF16)

        def hid_send(i, c):
            hid_copy(ch, i).start()
            return c

        lax.fori_loop(1, NZ, hid_send, 0)

    loads[2].wait()
    swaps[2].wait_recv()
    for ch, (lo, width) in enumerate(CHUNKS):
        for i in range(1, NZ):
            back = around(z, NZ, NZ - i)
            remote(
                hid[ch].at[back], hid[ch].at[back], hss.at[ch, i - 1], hrs.at[ch, i - 1], at(x, y, back, core)
            ).wait_recv()
        h = hid[ch][...].astype(F32).reshape(NZ * rows, width).astype(BF16)
        for cc in range(NC):
            term = jnp.dot(h, wd[cc, lo : lo + width], preferred_element_type=F32)
            part[cc] = term if ch == 0 else part[cc] + term

    def out_copy(i):
        dc, dy = i // NY, lax.rem(i, NY)
        return remote(
            send_c.at[i], recv_c.at[row], css.at[i], crs.at[row], at(core, around(y, NY, dy), z, around(core, NC, dc))
        )

    def out_send(i, c):
        dc, dy = i // NY, lax.rem(i, NY)
        send_c[i] = part[around(core, NC, dc), own_rows(around(y, NY, dy))].astype(BF16)
        own = jnp.logical_and(home, i == 0)

        @pl.when(own)
        def _():
            pltpu.make_async_copy(send_c.at[i], recv_c.at[row], crs.at[row]).start()

        @pl.when(jnp.logical_not(own))
        def _():
            out_copy(i).start()

        return c

    lax.fori_loop(0, NC * NY, out_send, 0)

    total = jnp.zeros(out.shape, F32)
    for i in range(NX * NY):
        pltpu.make_async_copy(send_c.at[0], recv_c.at[i], crs.at[i]).wait()
        total = total + recv_c[i].astype(F32)
    out[...] = total.astype(BF16)

    for copy in swaps:
        copy.wait_send()

    def row_sent(i, c):
        @pl.when(jnp.logical_not(jnp.logical_and(home, i == 0)))
        def _():
            tok_copy(i).wait_send()
            out_copy(i).wait_send()

        return c

    lax.fori_loop(0, NX * NY, row_sent, 0)
    for ch in range(len(CHUNKS)):

        def col_sent(i, c):
            sum_copy(ch, i).wait_send()
            hid_copy(ch, i).wait_send()
            return c

        lax.fori_loop(1, NZ, col_sent, 0)


def shards(tokens, gate_weight, up_weight, down_weight):
    rows, kd = tokens.shape
    ff, nd = down_weight.shape
    tall = NY * rows
    widths = [w for _, w in CHUNKS]
    dma = pltpu.SemaphoreType.DMA
    n = len(CHUNKS)
    return pl.pallas_call(
        kernel,
        out_shape=jax.ShapeDtypeStruct((rows, nd), BF16),
        in_specs=[pl.BlockSpec(memory_space=pl.ANY)] * 4,
        out_specs=pl.BlockSpec(memory_space=pltpu.VMEM),
        scratch_shapes=[
            pltpu.VMEM((NC * kd, ff), BF16),
            pltpu.VMEM((NC * kd, ff), BF16),
            pltpu.VMEM((NC, ff, nd), BF16),
            pltpu.VMEM((NY, NC, rows, kd), BF16),
            pltpu.VMEM((tall, ff), F32),
            pltpu.VMEM((tall, ff), F32),
            *[pltpu.VMEM((NZ - 1, 2 * rows, w), BF16) for w in widths],
            *[pltpu.VMEM((NZ - 1, 2 * rows, w), BF16) for w in widths],
            *[pltpu.VMEM((NZ, rows, w), BF16) for w in widths],
            pltpu.VMEM((NC, tall, nd), F32),
            pltpu.VMEM((NC * NY, rows, nd), BF16),
            pltpu.VMEM((NX * NY, rows, nd), BF16),
            dma((3,)), dma((3,)), dma((3,)),
            dma((NX * NY,)), dma((NY, NC)),
            dma((n, NZ - 1)), dma((n, NZ - 1)), dma((n, NZ - 1)), dma((n, NZ - 1)),
            dma((NC * NY,)), dma((NX * NY,)),
        ],
        compiler_params=pltpu.CompilerParams(collective_id=0, has_side_effects=True, vmem_limit_bytes=60 << 20),
        name="feed_forward",
    )(tokens, gate_weight, up_weight, down_weight)


def solution(mesh):
    in_specs = (P(("depth", "row"), "col"), P("col", "row"), P("col", "row"), P("row", "col"))
    out_specs = P(("depth", "row"), "col")
    return jax.shard_map(shards, mesh=mesh, in_specs=in_specs, out_specs=out_specs, check_vma=False)
```

```python
import jax
import jax.numpy as jnp
from jax import lax
from jax.experimental import pallas as pl
from jax.experimental.pallas import tpu as pltpu
from jax.sharding import PartitionSpec as P

MESH = pl.DeviceIdType.MESH
NX, NY, NZ, NC = 2, 8, 8, 2
NG = NX * NY
FAR = (4, 3, 5, 2, 6, 1, 7, 0)
TILE = 8
F32, BF16 = jnp.float32, jnp.bfloat16


def fold(v):
    half = v.shape[1] // 2
    return jnp.concatenate([v[:, :half], v[:, half:]], axis=0).astype(BF16)


def kernel(
    tok, gate, up, down, out,
    tok_in, wg, wu, wd, tok_own, tok_first, tok_rest, gate_sum, up_sum, send_b, recv_b, hid, part, send_c, recv_c,
    load_sem, wss, wrs, ass, ars, rss, rrs, fss, frs, bss, brs, hss, hrs, css, crs,
):
    depth, row, col = lax.axis_index("depth"), lax.axis_index("row"), lax.axis_index("col")
    x, y = row // NY, lax.rem(row, NY)
    z, core = col // NC, lax.rem(col, NC)
    rows, kd = tok.shape
    ff = gate.shape[1]
    chunks = rows // TILE
    home = x == core

    def at(xx, yy, zz, cc):
        return (depth, xx * NY + yy, zz * NC + cc)

    def around(v, n, by):
        return lax.rem(v + by, n)

    def zat(i):
        return lax.rem(z + NZ + jnp.where(core == 0, i, -i), NZ)

    def remote(src, dst, ss, rs, device):
        return pltpu.make_async_remote_copy(src, dst, ss, rs, device_id=device, device_id_type=MESH)

    def rows_of(i):
        return pl.ds(pl.multiple_of(i * TILE, TILE), TILE)

    mine = pl.ds(pl.multiple_of(core * kd, kd), kd)
    tok_load = pltpu.make_async_copy(tok, tok_in, load_sem.at[3])
    tok_load.start()
    loads = [
        pltpu.make_async_copy(gate, wg.at[mine], load_sem.at[0]),
        pltpu.make_async_copy(up, wu.at[mine], load_sem.at[1]),
        pltpu.make_async_copy(down, wd.at[core], load_sem.at[2]),
    ]
    for copy in loads:
        copy.start()

    barrier = pltpu.get_barrier_semaphore()

    def greet(device):
        pl.semaphore_signal(barrier, inc=1, device_id=device, device_id_type=MESH)

    for dy in FAR:
        yy = around(y, NY, dy)
        greet(at(1 - core, yy, z, x))
        greet(at(core, yy, z, 1 - x))
        if dy:
            greet(at(core, yy, z, x))
        else:

            @pl.when(jnp.logical_not(home))
            def _():
                greet(at(core, yy, z, x))

    for i in range(1, NZ):
        greet(at(x, y, around(z, NZ, i), core))
    other = at(x, y, z, 1 - core)
    tok_load.wait()
    for t in range(chunks):
        tok_own[t] = fold(tok_in[...].astype(F32)[t * TILE : (t + 1) * TILE])
    pl.semaphore_wait(barrier, 3 * NY + NZ - 1 - jnp.where(home, 1, 0))

    def first_copy(i):
        dx, dy = i // NY, lax.rem(i, NY)
        there = at(around(x, NX, dx), around(y, NY, dy), z, x)
        return remote(tok_own.at[0], tok_first.at[y, core], ass.at[i], ars.at[y, core], there)

    def rest_copy(dy):
        there = at(x, around(y, NY, dy), z, x)
        return remote(tok_own.at[1:], tok_rest.at[y, core], rss.at[dy], rrs.at[y, core], there)

    def forward_copy(yy):
        return remote(tok_rest.at[yy], tok_rest.at[yy], fss.at[yy], frs.at[yy], at(1 - x, y, z, core))

    def start_unless_own(dy, dx, copy, src, dst, sem):
        if dy or dx:
            copy.start()
            return

        @pl.when(home)
        def _():
            pltpu.make_async_copy(src, dst, sem).start()

        @pl.when(jnp.logical_not(home))
        def _():
            copy.start()

    swaps = [
        remote(gate, wg.at[mine], wss.at[0], wrs.at[0], other),
        remote(up, wu.at[mine], wss.at[1], wrs.at[1], other),
        remote(down, wd.at[core], wss.at[2], wrs.at[2], other),
    ]
    for dy in FAR:
        for dx in (1, 0):
            start_unless_own(
                dy, dx, first_copy(dx * NY + dy), tok_own.at[0], tok_first.at[y, core], ars.at[y, core]
            )
    for copy in swaps:
        copy.start()
    for dy in FAR:
        start_unless_own(dy, 0, rest_copy(dy), tok_own.at[1:], tok_rest.at[y, core], rrs.at[y, core])

    def forward():
        @pl.when(home)
        def _():
            for dy in reversed(FAR):
                yy = around(y, NY, dy)
                for cc in range(NC):
                    pltpu.make_async_copy(tok_own.at[1:], tok_rest.at[yy, cc], rrs.at[yy, cc]).wait()
                forward_copy(yy).start()

    def rest_wait():
        @pl.when(jnp.logical_not(home))
        def _():
            for yy in range(NY):
                forward_copy(yy).wait_recv()

    first = ((-1, -4), (-1, -2), (1, 3), (1, 1))
    then = ((-3, -3), (-1, -1), (2, 2))

    def sum_copy(t, j):
        step = (first + then)[j][0]
        return remote(
            send_b.at[t, j], recv_b.at[t, j], bss.at[t, j], brs.at[t, j], at(x, y, zat(step), core)
        )

    def own_part(t, who):
        there = rows_of(who)
        return jnp.concatenate([gate_sum[t, there], up_sum[t, there]], axis=0)

    def up_products(t):
        if t == 0:
            for yy in range(NY):
                for cc in range(NC):
                    pltpu.make_async_copy(tok_own.at[0], tok_first.at[yy, cc], ars.at[yy, cc]).wait()
            loads[0].wait()
            swaps[0].wait_recv()
            loads[1].wait()
            swaps[1].wait_recv()
        blocks = []
        for cc in range(NC):
            v = (tok_first[:, cc] if t == 0 else tok_rest[:, cc, t - 1]).astype(F32)
            blocks += [v[:, :TILE].reshape(NY * TILE, kd // 2), v[:, TILE:].reshape(NY * TILE, kd // 2)]
        lhs = jnp.concatenate(blocks, axis=1).astype(BF16)
        gate_sum[t] = jnp.dot(lhs, wg[...], preferred_element_type=F32)
        up_sum[t] = jnp.dot(lhs, wu[...], preferred_element_type=F32)
        for j, (_, who) in enumerate(first):
            send_b[t, j] = own_part(t, zat(who)).astype(BF16)
            sum_copy(t, j).start()

    def add_on_way(t):
        for k, (_, who) in enumerate(then):
            j = len(first) + k
            sum_copy(t, k).wait_recv()
            send_b[t, j] = (own_part(t, zat(who)) + recv_b[t, k].astype(F32)).astype(BF16)
            sum_copy(t, j).start()

    spread = ((3, 0), (1, 0), (-2, 0), (-1, 0))
    onward = ((1, -3), (1, -1), (-1, 2))

    def hid_copy(t, j):
        step, whose = (spread + onward)[j]
        block = hid.at[t, zat(whose)]
        return remote(block, block, hss.at[t, j], hrs.at[t, j], at(x, y, zat(step), core))

    def hid_arrived(t, j):
        step, whose = (spread + onward)[j]
        block = hid.at[t, zat(whose - step)]
        remote(block, block, hss.at[t, j], hrs.at[t, j], at(x, y, zat(step), core)).wait_recv()

    def hidden(t):
        both = own_part(t, z)
        for j in range(len(first) - 1, len(first) + len(then)):
            sum_copy(t, j).wait_recv()
            both = both + recv_b[t, j].astype(F32)
        h = jax.nn.silu(both[:TILE]) * both[TILE:]
        wide = hid.shape[3]
        right = jnp.concatenate([h[:, wide:], jnp.zeros((TILE, 2 * wide - ff), F32)], axis=1)
        hid[t, z] = jnp.concatenate([h[:, :wide], right], axis=0).astype(BF16)
        for j in range(len(spread)):
            hid_copy(t, j).start()

    def pass_on(t):
        for k in range(len(onward)):
            hid_arrived(t, k)
            hid_copy(t, len(spread) + k).start()

    def out_copy(t, i):
        dc, dy = i // NY, lax.rem(i, NY)
        there = at(core, around(y, NY, dy), z, around(core, NC, dc))
        return remote(send_c.at[t, i], recv_c.at[t, row], css.at[t, i], crs.at[t, row], there)

    def down_products(t):
        for j in range(len(spread) - 1, len(spread) + len(onward)):
            hid_arrived(t, j)
        if t == 0:
            loads[2].wait()
            swaps[2].wait_recv()
        v, wide = hid[t].astype(F32), hid.shape[3]
        left, right = v[:, :TILE].reshape(NZ * TILE, wide), v[:, TILE:].reshape(NZ * TILE, wide)
        h = jnp.concatenate([left, right[:, : ff - wide]], axis=1).astype(BF16)
        for cc in range(NC):
            part[cc] = jnp.dot(h, wd[cc], preferred_element_type=F32)

        for dy in FAR:
            for dc in (1, 0):
                i = dc * NY + dy
                send_c[t, i] = fold(part[around(core, NC, dc), rows_of(around(y, NY, dy))])
                start_unless_own(dy, dc, out_copy(t, i), send_c.at[t, i], recv_c.at[t, row], crs.at[t, row])

    def out_rows(t):
        total = jnp.zeros((2 * TILE, kd // 2), F32)
        for i in range(NG):
            pltpu.make_async_copy(send_c.at[t, 0], recv_c.at[t, i], crs.at[t, i]).wait()
            total = total + recv_c[t, i].astype(F32)
        return jnp.concatenate([total[:TILE], total[TILE:]], axis=1)

    def unless_own(copies):
        @pl.when(jnp.logical_not(home))
        def _():
            copies[0].wait_send()

        for copy in copies[1:]:
            copy.wait_send()

    up_products(0)
    forward()
    add_on_way(0)
    rest_wait()
    up_products(1)
    up_products(2)
    hidden(0)
    add_on_way(1)
    add_on_way(2)
    pass_on(0)
    hidden(1)
    hidden(2)
    down_products(0)
    pass_on(1)
    pass_on(2)
    down_products(1)
    down_products(2)

    for copy in swaps:
        copy.wait_send()
    unless_own([first_copy(i) for i in range(NG)])
    unless_own([rest_copy(dy) for dy in range(NY)])

    @pl.when(home)
    def _():
        for yy in range(NY):
            forward_copy(yy).wait_send()

    for t in range(chunks):
        for j in range(NZ - 1):
            sum_copy(t, j).wait_send()
            hid_copy(t, j).wait_send()
    blocks = []
    for t in range(chunks):
        unless_own([out_copy(t, i) for i in range(NG)])
        blocks.append(out_rows(t))
    out[...] = jnp.concatenate(blocks, axis=0).astype(BF16)


def shards(tokens, gate_weight, up_weight, down_weight):
    rows, kd = tokens.shape
    ff, nd = down_weight.shape
    n, tall = rows // TILE, NY * TILE
    wide = 512
    dma = pltpu.SemaphoreType.DMA
    return pl.pallas_call(
        kernel,
        out_shape=pltpu.VMEM((rows, nd), BF16),
        in_specs=[pl.BlockSpec(memory_space=pl.ANY)] * 4,
        out_specs=pl.BlockSpec(memory_space=pltpu.VMEM),
        scratch_shapes=[
            pltpu.VMEM((rows, kd), BF16),
            pltpu.VMEM((NC * kd, ff), BF16),
            pltpu.VMEM((NC * kd, ff), BF16),
            pltpu.VMEM((NC, ff, nd), BF16),
            pltpu.VMEM((n, 2 * TILE, kd // 2), BF16),
            pltpu.VMEM((NY, NC, 2 * TILE, kd // 2), BF16),
            pltpu.VMEM((NY, NC, n - 1, 2 * TILE, kd // 2), BF16),
            pltpu.VMEM((n, tall, ff), F32),
            pltpu.VMEM((n, tall, ff), F32),
            pltpu.VMEM((n, NZ - 1, 2 * TILE, ff), BF16),
            pltpu.VMEM((n, NZ - 1, 2 * TILE, ff), BF16),
            pltpu.VMEM((n, NZ, 2 * TILE, wide), BF16),
            pltpu.VMEM((NC, tall, nd), F32),
            pltpu.VMEM((n, NG, 2 * TILE, nd // 2), BF16),
            pltpu.VMEM((n, NG, 2 * TILE, nd // 2), BF16),
            dma((4,)), dma((3,)), dma((3,)),
            dma((NG,)), dma((NY, NC)), dma((NY,)), dma((NY, NC)), dma((NY,)), dma((NY,)),
            dma((n, NZ - 1)), dma((n, NZ - 1)), dma((n, NZ - 1)), dma((n, NZ - 1)),
            dma((n, NG)), dma((n, NG)),
        ],
        compiler_params=pltpu.CompilerParams(collective_id=0, has_side_effects=True, vmem_limit_bytes=60 << 20),
        name="feed_forward",
    )(tokens, gate_weight, up_weight, down_weight)


def solution(mesh):
    in_specs = (P(("depth", "row"), "col"), P("col", "row"), P("col", "row"), P("row", "col"))
    out_specs = P(("depth", "row"), "col")
    return jax.shard_map(shards, mesh=mesh, in_specs=in_specs, out_specs=out_specs, check_vma=False)
```

```python
import jax
import jax.numpy as jnp
from jax import lax
from jax.experimental import pallas as pl
from jax.experimental.pallas import tpu as pltpu
from jax.sharding import PartitionSpec as P

MESH = pl.DeviceIdType.MESH
NX, NY, NZ, NC = 2, 8, 8, 2
NG = NX * NY
CHUNKS = (
    ((0, 0, 3), (1, 0, 3), (7, 0, 2)),
    ((4, 0, 3), (3, 0, 3), (5, 0, 2)),
    ((7, 2, 1), (5, 2, 1), (2, 0, 3), (6, 0, 3)),
)
DIRECT = tuple((i, i) for i in (4, -3, 3, -2, 2, -1, 1))
SUM_TREE = (((-1, -4), (-1, -2), (1, 3), (1, 1)), ((-3, -3), (-1, -1), (2, 2)))
SUMS = ((DIRECT, ()), SUM_TREE, SUM_TREE)
SPREAD = tuple((i, 0) for i in (4, -3, 3, -2, 2, -1, 1))
HID_TREE = (((3, 0), (1, 0), (-2, 0), (-1, 0)), ((1, -3), (1, -1), (-1, 2)))
HIDS = ((SPREAD, ()), (SPREAD, ()), (SPREAD, ()))
ORDER = tuple(o for chunk in CHUNKS for o, tile, _ in chunk if tile == 0)
TILE = 8
F32, BF16 = jnp.float32, jnp.bfloat16


def fold(v):
    half = v.shape[1] // 2
    v = v.reshape(-1, TILE, 2 * half)
    return jnp.concatenate([v[:, :, :half], v[:, :, half:]], axis=1).astype(BF16)


def kernel(
    tok, gate, up, down, out,
    tok_in, wg, wu, wd, tok_own, tok_all, gate_sum, up_sum, send_b, recv_b, hid, part, send_c, recv_c,
    load_sem, wss, wrs, ass, ars, fss, frs, bss, brs, hss, hrs, css, crs,
):
    depth, row, col = lax.axis_index("depth"), lax.axis_index("row"), lax.axis_index("col")
    x, y = row // NY, lax.rem(row, NY)
    z, core = col // NC, lax.rem(col, NC)
    rows, kd = tok.shape
    ff = gate.shape[1]
    tiles, chunks = rows // TILE, len(CHUNKS)
    home = x == core

    def at(xx, yy, zz, cc):
        return (depth, xx * NY + yy, zz * NC + cc)

    def around(v, n, by):
        return lax.rem(v + by, n)

    def zat(i):
        return lax.rem(z + NZ + jnp.where(core == 0, i, -i), NZ)

    def remote(src, dst, ss, rs, device):
        return pltpu.make_async_remote_copy(src, dst, ss, rs, device_id=device, device_id_type=MESH)

    def rows_of(i):
        return pl.ds(pl.multiple_of(i * TILE, TILE), TILE)

    mine = pl.ds(pl.multiple_of(core * kd, kd), kd)
    tok_load = pltpu.make_async_copy(tok, tok_in, load_sem.at[3])
    tok_load.start()
    loads = [
        pltpu.make_async_copy(gate, wg.at[mine], load_sem.at[0]),
        pltpu.make_async_copy(up, wu.at[mine], load_sem.at[1]),
        pltpu.make_async_copy(down, wd.at[core], load_sem.at[2]),
    ]
    for copy in loads:
        copy.start()

    barrier = pltpu.get_barrier_semaphore()

    def greet(device):
        pl.semaphore_signal(barrier, inc=1, device_id=device, device_id_type=MESH)

    for o in ORDER:
        yy = around(y, NY, o)
        greet(at(1 - core, yy, z, x))
        greet(at(core, yy, z, 1 - x))
        if o:
            greet(at(core, yy, z, x))
        else:

            @pl.when(jnp.logical_not(home))
            def _():
                greet(at(core, yy, z, x))

    for i in range(1, NZ):
        greet(at(x, y, around(z, NZ, i), core))
    other = at(x, y, z, 1 - core)
    tok_load.wait()
    tok_own[...] = fold(tok_in[...].astype(F32))
    pl.semaphore_wait(barrier, 3 * NY + NZ - 1 - jnp.where(home, 1, 0))

    def tok_copy(o, dx):
        there = at(around(x, NX, dx), around(y, NY, NY - o), z, x)
        return remote(tok_own, tok_all.at[y, core], ass.at[dx, o], ars.at[y, core], there)

    def tok_sends(t):
        for o, tile, _ in CHUNKS[t]:
            for dx in (1, 0) if t == 0 else (0,):
                if tile == 0:
                    start_unless_own(o, dx, tok_copy(o, dx), tok_own, tok_all.at[y, core], ars.at[y, core])

    def forward_copy(yy):
        return remote(tok_all.at[yy], tok_all.at[yy], fss.at[yy], frs.at[yy], at(1 - x, y, z, core))

    def tok_wait(yy):
        for cc in range(NC):
            pltpu.make_async_copy(tok_own, tok_all.at[yy, cc], ars.at[yy, cc]).wait()

    def forward(t):
        @pl.when(home)
        def _():
            for o, tile, _ in CHUNKS[t]:
                if tile == 0:
                    yy = around(y, NY, o)
                    tok_wait(yy)
                    forward_copy(yy).start()

    def start_unless_own(dy, dx, copy, src, dst, sem):
        if dy or dx:
            copy.start()
            return

        @pl.when(home)
        def _():
            pltpu.make_async_copy(src, dst, sem).start()

        @pl.when(jnp.logical_not(home))
        def _():
            copy.start()

    swaps = [
        remote(gate, wg.at[mine], wss.at[0], wrs.at[0], other),
        remote(up, wu.at[mine], wss.at[1], wrs.at[1], other),
        remote(down, wd.at[core], wss.at[2], wrs.at[2], other),
    ]
    tok_sends(0)
    for copy in swaps:
        copy.start()
    for t in range(1, chunks):
        tok_sends(t)

    def sum_copy(t, j):
        step = (SUMS[t][0] + SUMS[t][1])[j][0]
        return remote(
            send_b.at[t, j], recv_b.at[t, j], bss.at[t, j], brs.at[t, j], at(x, y, zat(step), core)
        )

    def own_part(t, who):
        there = rows_of(who)
        return jnp.concatenate([gate_sum[t, there], up_sum[t, there]], axis=0)

    def up_products(t):
        blocks = []
        for o, tile, n in CHUNKS[t]:
            yy = around(y, NY, o)
            if tile == 0:
                if t == 0:
                    tok_wait(yy)
                else:

                    @pl.when(jnp.logical_not(home))
                    def _():
                        forward_copy(yy).wait_recv()

            parts = []
            for cc in range(NC):
                v = tok_all[yy, cc, tile : tile + n].astype(F32)
                parts += [v[:, :TILE].reshape(n * TILE, kd // 2), v[:, TILE:].reshape(n * TILE, kd // 2)]
            blocks.append(jnp.concatenate(parts, axis=1))
        if t == 0:
            loads[0].wait()
            swaps[0].wait_recv()
            loads[1].wait()
            swaps[1].wait_recv()
        lhs = jnp.concatenate(blocks, axis=0).astype(BF16)
        gate_sum[t] = jnp.dot(lhs, wg[...], preferred_element_type=F32)
        up_sum[t] = jnp.dot(lhs, wu[...], preferred_element_type=F32)
        for j, (_, who) in enumerate(SUMS[t][0]):
            send_b[t, j] = own_part(t, zat(who)).astype(BF16)
            sum_copy(t, j).start()

    def add_on_way(t):
        for k, (_, who) in enumerate(SUMS[t][1]):
            j = len(SUMS[t][0]) + k
            sum_copy(t, k).wait_recv()
            send_b[t, j] = (own_part(t, zat(who)) + recv_b[t, k].astype(F32)).astype(BF16)
            sum_copy(t, j).start()

    def hid_copy(t, j):
        step, whose = (HIDS[t][0] + HIDS[t][1])[j]
        block = hid.at[t, zat(whose)]
        return remote(block, block, hss.at[t, j], hrs.at[t, j], at(x, y, zat(step), core))

    def hid_arrived(t, j):
        step, whose = (HIDS[t][0] + HIDS[t][1])[j]
        block = hid.at[t, zat(whose - step)]
        remote(block, block, hss.at[t, j], hrs.at[t, j], at(x, y, zat(step), core)).wait_recv()

    def hidden(t):
        both = own_part(t, z)
        for j in range(len(SUMS[t][1]), NZ - 1):
            sum_copy(t, j).wait_recv()
            both = both + recv_b[t, j].astype(F32)
        h = jax.nn.silu(both[:TILE]) * both[TILE:]
        hid[t, z] = h.astype(BF16)
        for j in range(len(HIDS[t][0])):
            hid_copy(t, j).start()

    def pass_on(t):
        for k in range(len(HIDS[t][1])):
            hid_arrived(t, k)
            hid_copy(t, len(HIDS[t][0]) + k).start()

    def out_copy(o, tile, n, dc):
        there = at(core, around(y, NY, o), z, around(core, NC, dc))
        return remote(
            send_c.at[dc, o, tile : tile + n], recv_c.at[row, tile : tile + n],
            css.at[dc, o, tile], crs.at[row, tile], there,
        )

    def down_products(t):
        for j in range(len(HIDS[t][1]), NZ - 1):
            hid_arrived(t, j)
        if t == 0:
            loads[2].wait()
            swaps[2].wait_recv()
        h = hid[t].astype(F32).reshape(NZ * TILE, ff).astype(BF16)
        for cc in range(NC):
            part[cc] = jnp.dot(h, wd[cc], preferred_element_type=F32)

        at_tile = 0
        for o, tile, n in CHUNKS[t]:
            for dc in (1, 0):
                term = part[around(core, NC, dc), at_tile * TILE : (at_tile + n) * TILE]
                send_c[dc, o, tile : tile + n] = fold(term)
                here = pl.ds(tile, n)
                start_unless_own(
                    o, dc, out_copy(o, tile, n, dc), send_c.at[dc, o, here], recv_c.at[row, here],
                    crs.at[row, tile],
                )
            at_tile += n

    def unless_own(copies):
        @pl.when(jnp.logical_not(home))
        def _():
            copies[0].wait_send()

        for copy in copies[1:]:
            copy.wait_send()

    up_products(0)
    forward(1)
    forward(2)
    add_on_way(0)
    up_products(1)
    up_products(2)
    add_on_way(1)
    hidden(0)
    add_on_way(2)
    hidden(1)
    hidden(2)
    down_products(0)
    down_products(1)
    down_products(2)

    for copy in swaps:
        copy.wait_send()
    near = [o for o, _, _ in CHUNKS[0]]
    unless_own([tok_copy(o, dx) for o in range(NY) for dx in range(NX if o in near else 1)])

    @pl.when(home)
    def _():
        for o in ORDER[len(near) :]:
            forward_copy(around(y, NY, o)).wait_send()

    for t in range(chunks):
        for j in range(NZ - 1):
            sum_copy(t, j).wait_send()
            hid_copy(t, j).wait_send()
    unless_own([out_copy(o, tile, n, dc) for o, tile, n in sorted(sum(CHUNKS, ())) for dc in range(NC)])

    total = jnp.zeros(recv_c.shape[1:], F32)
    for chunk in CHUNKS:
        for o, tile, n in chunk:
            for xx in range(NX):
                source = xx * NY + around(y, NY, NY - o)
                here = pl.ds(tile, n)
                pltpu.make_async_copy(
                    send_c.at[0, 0, here], recv_c.at[source, here], crs.at[source, tile]
                ).wait()
    for i in range(NG):
        total = total + recv_c[i].astype(F32)
    total = jnp.concatenate([total[:, :TILE], total[:, TILE:]], axis=2)
    out[...] = total.reshape(out.shape).astype(BF16)


def shards(tokens, gate_weight, up_weight, down_weight):
    rows, kd = tokens.shape
    ff, nd = down_weight.shape
    n, tiles, tall = len(CHUNKS), rows // TILE, NY * TILE
    dma = pltpu.SemaphoreType.DMA
    return pl.pallas_call(
        kernel,
        out_shape=pltpu.VMEM((rows, nd), BF16),
        in_specs=[pl.BlockSpec(memory_space=pl.ANY)] * 4,
        out_specs=pl.BlockSpec(memory_space=pltpu.VMEM),
        scratch_shapes=[
            pltpu.VMEM((rows, kd), BF16),
            pltpu.VMEM((NC * kd, ff), BF16),
            pltpu.VMEM((NC * kd, ff), BF16),
            pltpu.VMEM((NC, ff, nd), BF16),
            pltpu.VMEM((tiles, 2 * TILE, kd // 2), BF16),
            pltpu.VMEM((NY, NC, tiles, 2 * TILE, kd // 2), BF16),
            pltpu.VMEM((n, tall, ff), F32),
            pltpu.VMEM((n, tall, ff), F32),
            pltpu.VMEM((n, NZ - 1, 2 * TILE, ff), BF16),
            pltpu.VMEM((n, NZ - 1, 2 * TILE, ff), BF16),
            pltpu.VMEM((n, NZ, TILE, ff), BF16),
            pltpu.VMEM((NC, tall, nd), F32),
            pltpu.VMEM((NC, NY, tiles, 2 * TILE, nd // 2), BF16),
            pltpu.VMEM((NG, tiles, 2 * TILE, nd // 2), BF16),
            dma((4,)), dma((3,)), dma((3,)),
            dma((NX, NY)), dma((NY, NC)), dma((NY,)), dma((NY,)),
            dma((n, NZ - 1)), dma((n, NZ - 1)), dma((n, NZ - 1)), dma((n, NZ - 1)),
            dma((NC, NY, tiles)), dma((NG, tiles)),
        ],
        compiler_params=pltpu.CompilerParams(collective_id=0, has_side_effects=True, vmem_limit_bytes=60 << 20),
        name="feed_forward",
    )(tokens, gate_weight, up_weight, down_weight)


def solution(mesh):
    in_specs = (P(("depth", "row"), "col"), P("col", "row"), P("col", "row"), P("row", "col"))
    out_specs = P(("depth", "row"), "col")
    return jax.shard_map(shards, mesh=mesh, in_specs=in_specs, out_specs=out_specs, check_vma=False)
```

```python
import jax
import jax.numpy as jnp
from jax import lax
from jax.experimental import pallas as pl
from jax.experimental.pallas import tpu as pltpu
from jax.sharding import PartitionSpec as P

MESH = pl.DeviceIdType.MESH
NX, NY, NZ, NC = 2, 8, 8, 2
NG = NX * NY
CHUNKS = (
    ((0, 0, 3), (1, 0, 3), (7, 0, 2)),
    ((4, 0, 3), (3, 0, 3), (5, 0, 2)),
    ((5, 2, 1), (2, 0, 3), (6, 0, 3), (7, 2, 1)),
)
DIRECT = tuple((i, i) for i in (4, -3, 3, -2, 2, -1, 1))
SUM_TREE = (((-1, -4), (-1, -2), (1, 3), (1, 1)), ((-3, -3), (-1, -1), (2, 2)))
SUMS = ((DIRECT, ()), SUM_TREE, SUM_TREE)
SPREAD = tuple((i, 0) for i in (4, -3, 3, -2, 2, -1, 1))
HID_TREE = (((3, 0), (1, 0), (-2, 0), (-1, 0)), ((1, -3), (1, -1), (-1, 2)))
HIDS = ((SPREAD, ()), (SPREAD, ()), (SPREAD, ()))
ORDER = tuple(o for chunk in CHUNKS for o, tile, _ in chunk if tile == 0)
TILE = 8
F32, BF16 = jnp.float32, jnp.bfloat16


def fold(v):
    half = v.shape[1] // 2
    v = v.reshape(-1, TILE, 2 * half)
    return jnp.concatenate([v[:, :, :half], v[:, :, half:]], axis=1).astype(BF16)


def kernel(
    tok, gate, up, down, out,
    tok_in, wg, wu, wd, tok_own, tok_all, gate_sum, up_sum, send_b, recv_b, hid, part, send_c, recv_c,
    load_sem, wss, wrs, ass, ars, fss, frs, bss, brs, hss, hrs, css, crs,
):
    depth, row, col = lax.axis_index("depth"), lax.axis_index("row"), lax.axis_index("col")
    x, y = row // NY, lax.rem(row, NY)
    z, core = col // NC, lax.rem(col, NC)
    rows, kd = tok.shape
    ff = gate.shape[1]
    tiles, chunks = rows // TILE, len(CHUNKS)
    home = x == core

    def at(xx, yy, zz, cc):
        return (depth, xx * NY + yy, zz * NC + cc)

    def around(v, n, by):
        return lax.rem(v + by, n)

    def zat(i):
        return lax.rem(z + NZ + jnp.where(core == 0, i, -i), NZ)

    def remote(src, dst, ss, rs, device):
        return pltpu.make_async_remote_copy(src, dst, ss, rs, device_id=device, device_id_type=MESH)

    def rows_of(i):
        return pl.ds(pl.multiple_of(i * TILE, TILE), TILE)

    mine = pl.ds(pl.multiple_of(core * kd, kd), kd)
    tok_load = pltpu.make_async_copy(tok, tok_in, load_sem.at[3])
    tok_load.start()
    loads = [
        pltpu.make_async_copy(gate, wg.at[mine], load_sem.at[0]),
        pltpu.make_async_copy(up, wu.at[mine], load_sem.at[1]),
        pltpu.make_async_copy(down, wd.at[core], load_sem.at[2]),
    ]
    for copy in loads:
        copy.start()

    barrier = pltpu.get_barrier_semaphore()

    def greet(device):
        pl.semaphore_signal(barrier, inc=1, device_id=device, device_id_type=MESH)

    for o in ORDER:
        yy = around(y, NY, o)
        greet(at(1 - core, yy, z, x))
        greet(at(core, yy, z, 1 - x))
        if o:
            greet(at(core, yy, z, x))
        else:

            @pl.when(jnp.logical_not(home))
            def _():
                greet(at(core, yy, z, x))

    for i in range(1, NZ):
        greet(at(x, y, around(z, NZ, i), core))
    other = at(x, y, z, 1 - core)
    tok_load.wait()
    tok_own[...] = fold(tok_in[...].astype(F32))
    pl.semaphore_wait(barrier, 3 * NY + NZ - 1 - jnp.where(home, 1, 0))

    def tok_copy(o, dx):
        there = at(around(x, NX, dx), around(y, NY, NY - o), z, x)
        return remote(tok_own, tok_all.at[y, core], ass.at[dx, o], ars.at[y, core], there)

    def tok_sends(t):
        for o, tile, _ in CHUNKS[t]:
            for dx in (1, 0) if t == 0 else (0,):
                if tile == 0:
                    start_unless_own(o, dx, tok_copy(o, dx), tok_own, tok_all.at[y, core], ars.at[y, core])

    def forward_copy(yy):
        return remote(tok_all.at[yy], tok_all.at[yy], fss.at[yy], frs.at[yy], at(1 - x, y, z, core))

    def tok_wait(yy):
        for cc in range(NC):
            pltpu.make_async_copy(tok_own, tok_all.at[yy, cc], ars.at[yy, cc]).wait()

    def forward(t):
        @pl.when(home)
        def _():
            for o, tile, _ in CHUNKS[t]:
                if tile == 0:
                    yy = around(y, NY, o)
                    tok_wait(yy)
                    forward_copy(yy).start()

    def start_unless_own(dy, dx, copy, src, dst, sem):
        if dy or dx:
            copy.start()
            return

        @pl.when(home)
        def _():
            pltpu.make_async_copy(src, dst, sem).start()

        @pl.when(jnp.logical_not(home))
        def _():
            copy.start()

    swaps = [
        remote(gate, wg.at[mine], wss.at[0], wrs.at[0], other),
        remote(up, wu.at[mine], wss.at[1], wrs.at[1], other),
        remote(down, wd.at[core], wss.at[2], wrs.at[2], other),
    ]
    tok_sends(0)
    for copy in swaps:
        copy.start()
    for t in range(1, chunks):
        tok_sends(t)

    def sum_copy(t, j):
        step = (SUMS[t][0] + SUMS[t][1])[j][0]
        return remote(
            send_b.at[t, j], recv_b.at[t, j], bss.at[t, j], brs.at[t, j], at(x, y, zat(step), core)
        )

    def own_part(t, who):
        there = rows_of(who)
        return jnp.concatenate([gate_sum[t, there], up_sum[t, there]], axis=0)

    def up_products(t):
        blocks = []
        for o, tile, n in CHUNKS[t]:
            yy = around(y, NY, o)
            if tile == 0:
                if t == 0:
                    tok_wait(yy)
                else:

                    @pl.when(jnp.logical_not(home))
                    def _():
                        forward_copy(yy).wait_recv()

            parts = []
            for cc in range(NC):
                v = tok_all[yy, cc, tile : tile + n].astype(F32)
                parts += [v[:, :TILE].reshape(n * TILE, kd // 2), v[:, TILE:].reshape(n * TILE, kd // 2)]
            blocks.append(jnp.concatenate(parts, axis=1))
        if t == 0:
            loads[0].wait()
            swaps[0].wait_recv()
            loads[1].wait()
            swaps[1].wait_recv()
        lhs = jnp.concatenate(blocks, axis=0).astype(BF16)
        gate_sum[t] = jnp.dot(lhs, wg[...], preferred_element_type=F32)
        up_sum[t] = jnp.dot(lhs, wu[...], preferred_element_type=F32)
        for j, (_, who) in enumerate(SUMS[t][0]):
            send_b[t, j] = own_part(t, zat(who)).astype(BF16)
            sum_copy(t, j).start()

    def add_on_way(t):
        for k, (_, who) in enumerate(SUMS[t][1]):
            j = len(SUMS[t][0]) + k
            sum_copy(t, k).wait_recv()
            send_b[t, j] = (own_part(t, zat(who)) + recv_b[t, k].astype(F32)).astype(BF16)
            sum_copy(t, j).start()

    def hid_copy(t, j):
        step, whose = (HIDS[t][0] + HIDS[t][1])[j]
        block = hid.at[t, zat(whose)]
        return remote(block, block, hss.at[t, j], hrs.at[t, j], at(x, y, zat(step), core))

    def hid_arrived(t, j):
        step, whose = (HIDS[t][0] + HIDS[t][1])[j]
        block = hid.at[t, zat(whose - step)]
        remote(block, block, hss.at[t, j], hrs.at[t, j], at(x, y, zat(step), core)).wait_recv()

    def hidden(t):
        both = own_part(t, z)
        for j in range(len(SUMS[t][1]), NZ - 1):
            sum_copy(t, j).wait_recv()
            both = both + recv_b[t, j].astype(F32)
        h = jax.nn.silu(both[:TILE]) * both[TILE:]
        hid[t, z] = h.astype(BF16)
        for j in range(len(HIDS[t][0])):
            hid_copy(t, j).start()

    def pass_on(t):
        for k in range(len(HIDS[t][1])):
            hid_arrived(t, k)
            hid_copy(t, len(HIDS[t][0]) + k).start()

    def out_copy(o, tile, n, dc):
        there = at(core, around(y, NY, o), z, around(core, NC, dc))
        return remote(
            send_c.at[dc, o, tile : tile + n], recv_c.at[row, tile : tile + n],
            css.at[dc, o, tile], crs.at[row, tile], there,
        )

    def down_products(t):
        for j in range(len(HIDS[t][1]), NZ - 1):
            hid_arrived(t, j)
        h = hid[t].astype(F32).reshape(NZ * TILE, ff).astype(BF16)
        for cc in range(NC):
            part[cc] = jnp.dot(h, wd[cc], preferred_element_type=F32)

        at_tile = 0
        for o, tile, n in CHUNKS[t]:
            for dc in (1, 0):
                term = part[around(core, NC, dc), at_tile * TILE : (at_tile + n) * TILE]
                send_c[dc, o, tile : tile + n] = fold(term)
                here = pl.ds(tile, n)
                start_unless_own(
                    o, dc, out_copy(o, tile, n, dc), send_c.at[dc, o, here], recv_c.at[row, here],
                    crs.at[row, tile],
                )
            at_tile += n

    def unless_own(copies):
        @pl.when(jnp.logical_not(home))
        def _():
            copies[0].wait_send()

        for copy in copies[1:]:
            copy.wait_send()

    up_products(0)
    forward(1)
    forward(2)
    up_products(1)
    up_products(2)
    add_on_way(1)
    add_on_way(2)
    hidden(1)
    hidden(0)
    hidden(2)
    loads[2].wait()
    swaps[2].wait_recv()
    down_products(1)
    down_products(0)
    down_products(2)

    for copy in swaps:
        copy.wait_send()
    near = [o for o, _, _ in CHUNKS[0]]
    unless_own([tok_copy(o, dx) for o in range(NY) for dx in range(NX if o in near else 1)])

    @pl.when(home)
    def _():
        for o in ORDER[len(near) :]:
            forward_copy(around(y, NY, o)).wait_send()

    for t in range(chunks):
        for j in range(NZ - 1):
            sum_copy(t, j).wait_send()
            hid_copy(t, j).wait_send()
    unless_own([out_copy(o, tile, n, dc) for o, tile, n in sorted(sum(CHUNKS, ())) for dc in range(NC)])

    total = jnp.zeros(recv_c.shape[1:], F32)
    for chunk in CHUNKS:
        for o, tile, n in chunk:
            for xx in range(NX):
                source = xx * NY + around(y, NY, NY - o)
                here = pl.ds(tile, n)
                pltpu.make_async_copy(
                    send_c.at[0, 0, here], recv_c.at[source, here], crs.at[source, tile]
                ).wait()
    for i in range(NG):
        total = total + recv_c[i].astype(F32)
    total = jnp.concatenate([total[:, :TILE], total[:, TILE:]], axis=2)
    out[...] = total.reshape(out.shape).astype(BF16)


def shards(tokens, gate_weight, up_weight, down_weight):
    rows, kd = tokens.shape
    ff, nd = down_weight.shape
    n, tiles, tall = len(CHUNKS), rows // TILE, NY * TILE
    dma = pltpu.SemaphoreType.DMA
    return pl.pallas_call(
        kernel,
        out_shape=pltpu.VMEM((rows, nd), BF16),
        in_specs=[pl.BlockSpec(memory_space=pl.ANY)] * 4,
        out_specs=pl.BlockSpec(memory_space=pltpu.VMEM),
        scratch_shapes=[
            pltpu.VMEM((rows, kd), BF16),
            pltpu.VMEM((NC * kd, ff), BF16),
            pltpu.VMEM((NC * kd, ff), BF16),
            pltpu.VMEM((NC, ff, nd), BF16),
            pltpu.VMEM((tiles, 2 * TILE, kd // 2), BF16),
            pltpu.VMEM((NY, NC, tiles, 2 * TILE, kd // 2), BF16),
            pltpu.VMEM((n, tall, ff), F32),
            pltpu.VMEM((n, tall, ff), F32),
            pltpu.VMEM((n, NZ - 1, 2 * TILE, ff), BF16),
            pltpu.VMEM((n, NZ - 1, 2 * TILE, ff), BF16),
            pltpu.VMEM((n, NZ, TILE, ff), BF16),
            pltpu.VMEM((NC, tall, nd), F32),
            pltpu.VMEM((NC, NY, tiles, 2 * TILE, nd // 2), BF16),
            pltpu.VMEM((NG, tiles, 2 * TILE, nd // 2), BF16),
            dma((4,)), dma((3,)), dma((3,)),
            dma((NX, NY)), dma((NY, NC)), dma((NY,)), dma((NY,)),
            dma((n, NZ - 1)), dma((n, NZ - 1)), dma((n, NZ - 1)), dma((n, NZ - 1)),
            dma((NC, NY, tiles)), dma((NG, tiles)),
        ],
        compiler_params=pltpu.CompilerParams(collective_id=0, has_side_effects=True, vmem_limit_bytes=60 << 20),
        name="feed_forward",
    )(tokens, gate_weight, up_weight, down_weight)


def solution(mesh):
    in_specs = (P(("depth", "row"), "col"), P("col", "row"), P("col", "row"), P("row", "col"))
    out_specs = P(("depth", "row"), "col")
    return jax.shard_map(shards, mesh=mesh, in_specs=in_specs, out_specs=out_specs, check_vma=False)
```

```python
import jax
import jax.numpy as jnp
from jax import lax
from jax.experimental import pallas as pl
from jax.experimental.pallas import tpu as pltpu
from jax.sharding import PartitionSpec as P

MESH = pl.DeviceIdType.MESH
NX, NY, NZ, NC = 2, 8, 8, 2
NG = NX * NY
CHUNKS = (
    ((0, 0, 3), (1, 0, 3), (7, 0, 2)),
    ((4, 0, 3), (3, 0, 3), (5, 0, 2)),
    ((5, 2, 1), (2, 0, 3), (6, 0, 3), (7, 2, 1)),
)
DIRECT = tuple((i, i) for i in (4, -3, 3, -2, 2, -1, 1))
SUM_TREE = (((-1, -4), (-1, -2), (1, 3), (1, 1)), ((-3, -3), (-1, -1), (2, 2)))
SUMS = ((DIRECT, ()), SUM_TREE, SUM_TREE)
SPREAD = tuple((i, 0) for i in (4, -3, 3, -2, 2, -1, 1))
HID_TREE = (((3, 0), (1, 0), (-2, 0), (-1, 0)), ((1, -3), (1, -1), (-1, 2)))
HIDS = ((SPREAD, ()), (SPREAD, ()), (SPREAD, ()))
ORDER = tuple(o for chunk in CHUNKS for o, tile, _ in chunk if tile == 0)
TILE = 8
F32, BF16 = jnp.float32, jnp.bfloat16


def fold(v):
    half = v.shape[1] // 2
    v = v.reshape(-1, TILE, 2 * half)
    return jnp.concatenate([v[:, :, :half], v[:, :, half:]], axis=1).astype(BF16)


def kernel(
    tok, gate, up, down, out,
    tok_in, wg, wu, wd, tok_own, tok_all, gate_sum, up_sum, send_b, recv_b, hid, part, send_c, recv_c,
    load_sem, wss, wrs, ass, ars, fss, frs, bss, brs, hss, hrs, css, crs,
):
    depth, row, col = lax.axis_index("depth"), lax.axis_index("row"), lax.axis_index("col")
    x, y = row // NY, lax.rem(row, NY)
    z, core = col // NC, lax.rem(col, NC)
    rows, kd = tok.shape
    ff = gate.shape[1]
    tiles, chunks = rows // TILE, len(CHUNKS)
    home = x == core

    def at(xx, yy, zz, cc):
        return (depth, xx * NY + yy, zz * NC + cc)

    def around(v, n, by):
        return lax.rem(v + by, n)

    def zat(i):
        return lax.rem(z + NZ + jnp.where(core == 0, i, -i), NZ)

    def remote(src, dst, ss, rs, device):
        return pltpu.make_async_remote_copy(src, dst, ss, rs, device_id=device, device_id_type=MESH)

    def rows_of(i):
        return pl.ds(pl.multiple_of(i * TILE, TILE), TILE)

    mine = pl.ds(pl.multiple_of(core * kd, kd), kd)
    tok_load = pltpu.make_async_copy(tok, tok_in, load_sem.at[3])
    tok_load.start()
    loads = [
        pltpu.make_async_copy(gate, wg.at[mine], load_sem.at[0]),
        pltpu.make_async_copy(up, wu.at[mine], load_sem.at[1]),
        pltpu.make_async_copy(down, wd.at[core], load_sem.at[2]),
    ]
    for copy in loads:
        copy.start()

    barrier = pltpu.get_barrier_semaphore()

    def greet(device):
        pl.semaphore_signal(barrier, inc=1, device_id=device, device_id_type=MESH)

    for o in ORDER:
        yy = around(y, NY, o)
        greet(at(1 - core, yy, z, x))
        greet(at(core, yy, z, 1 - x))
        if o:
            greet(at(core, yy, z, x))
        else:

            @pl.when(jnp.logical_not(home))
            def _():
                greet(at(core, yy, z, x))

    for i in range(1, NZ):
        greet(at(x, y, around(z, NZ, i), core))
    other = at(x, y, z, 1 - core)
    tok_load.wait()
    tok_own[...] = fold(tok_in[...].astype(F32))
    pl.semaphore_wait(barrier, 3 * NY + NZ - 1 - jnp.where(home, 1, 0))

    def tok_copy(o, dx):
        there = at(around(x, NX, dx), around(y, NY, NY - o), z, x)
        return remote(tok_own, tok_all.at[y, core], ass.at[dx, o], ars.at[y, core], there)

    def tok_sends(t):
        for o, tile, _ in CHUNKS[t]:
            for dx in (1, 0) if t == 0 else (0,):
                if tile == 0:
                    start_unless_own(o, dx, tok_copy(o, dx), tok_own, tok_all.at[y, core], ars.at[y, core])

    def forward_copy(yy):
        return remote(tok_all.at[yy], tok_all.at[yy], fss.at[yy], frs.at[yy], at(1 - x, y, z, core))

    def tok_wait(yy):
        for cc in range(NC):
            pltpu.make_async_copy(tok_own, tok_all.at[yy, cc], ars.at[yy, cc]).wait()

    def forward(t):
        @pl.when(home)
        def _():
            for o, tile, _ in CHUNKS[t]:
                if tile == 0:
                    yy = around(y, NY, o)
                    tok_wait(yy)
                    forward_copy(yy).start()

    def start_unless_own(dy, dx, copy, src, dst, sem):
        if dy or dx:
            copy.start()
            return

        @pl.when(home)
        def _():
            pltpu.make_async_copy(src, dst, sem).start()

        @pl.when(jnp.logical_not(home))
        def _():
            copy.start()

    swaps = [
        remote(gate, wg.at[mine], wss.at[0], wrs.at[0], other),
        remote(up, wu.at[mine], wss.at[1], wrs.at[1], other),
        remote(down, wd.at[core], wss.at[2], wrs.at[2], other),
    ]
    tok_sends(0)
    for copy in swaps:
        copy.start()
    tok_sends(2)
    tok_sends(1)

    def sum_copy(t, j):
        step = (SUMS[t][0] + SUMS[t][1])[j][0]
        return remote(
            send_b.at[t, j], recv_b.at[t, j], bss.at[t, j], brs.at[t, j], at(x, y, zat(step), core)
        )

    def own_part(t, who):
        there = rows_of(who)
        return jnp.concatenate([gate_sum[t, there], up_sum[t, there]], axis=0)

    def up_products(t):
        blocks = []
        for o, tile, n in CHUNKS[t]:
            yy = around(y, NY, o)
            if tile == 0:
                if t == 0:
                    tok_wait(yy)
                else:

                    @pl.when(jnp.logical_not(home))
                    def _():
                        forward_copy(yy).wait_recv()

            parts = []
            for cc in range(NC):
                v = tok_all[yy, cc, tile : tile + n].astype(F32)
                parts += [v[:, :TILE].reshape(n * TILE, kd // 2), v[:, TILE:].reshape(n * TILE, kd // 2)]
            blocks.append(jnp.concatenate(parts, axis=1))
        if t == 0:
            loads[0].wait()
            swaps[0].wait_recv()
            loads[1].wait()
            swaps[1].wait_recv()
        lhs = jnp.concatenate(blocks, axis=0).astype(BF16)
        gate_sum[t] = jnp.dot(lhs, wg[...], preferred_element_type=F32)
        up_sum[t] = jnp.dot(lhs, wu[...], preferred_element_type=F32)
        for j, (_, who) in enumerate(SUMS[t][0]):
            send_b[t, j] = own_part(t, zat(who)).astype(BF16)
            sum_copy(t, j).start()

    def add_on_way(t):
        for k, (_, who) in enumerate(SUMS[t][1]):
            j = len(SUMS[t][0]) + k
            sum_copy(t, k).wait_recv()
            send_b[t, j] = (own_part(t, zat(who)) + recv_b[t, k].astype(F32)).astype(BF16)
            sum_copy(t, j).start()

    def hid_copy(t, j):
        step, whose = (HIDS[t][0] + HIDS[t][1])[j]
        block = hid.at[t, zat(whose)]
        return remote(block, block, hss.at[t, j], hrs.at[t, j], at(x, y, zat(step), core))

    def hid_arrived(t, j):
        step, whose = (HIDS[t][0] + HIDS[t][1])[j]
        block = hid.at[t, zat(whose - step)]
        remote(block, block, hss.at[t, j], hrs.at[t, j], at(x, y, zat(step), core)).wait_recv()

    def hidden(t):
        both = own_part(t, z)
        for j in range(len(SUMS[t][1]), NZ - 1):
            sum_copy(t, j).wait_recv()
            both = both + recv_b[t, j].astype(F32)
        h = jax.nn.silu(both[:TILE]) * both[TILE:]
        hid[t, z] = h.astype(BF16)
        for j in range(len(HIDS[t][0])):
            hid_copy(t, j).start()

    def pass_on(t):
        for k in range(len(HIDS[t][1])):
            hid_arrived(t, k)
            hid_copy(t, len(HIDS[t][0]) + k).start()

    def out_copy(o, tile, n, dc):
        there = at(core, around(y, NY, o), z, around(core, NC, dc))
        return remote(
            send_c.at[dc, o, tile : tile + n], recv_c.at[row, tile : tile + n],
            css.at[dc, o, tile], crs.at[row, tile], there,
        )

    def down_products(t):
        for j in range(len(HIDS[t][1]), NZ - 1):
            hid_arrived(t, j)
        h = hid[t].astype(F32).reshape(NZ * TILE, ff).astype(BF16)
        for cc in range(NC):
            part[cc] = jnp.dot(h, wd[cc], preferred_element_type=F32)

        at_tile = 0
        for o, tile, n in CHUNKS[t]:
            for dc in (1, 0):
                term = part[around(core, NC, dc), at_tile * TILE : (at_tile + n) * TILE]
                send_c[dc, o, tile : tile + n] = fold(term)
                here = pl.ds(tile, n)
                start_unless_own(
                    o, dc, out_copy(o, tile, n, dc), send_c.at[dc, o, here], recv_c.at[row, here],
                    crs.at[row, tile],
                )
            at_tile += n

    def unless_own(copies):
        @pl.when(jnp.logical_not(home))
        def _():
            copies[0].wait_send()

        for copy in copies[1:]:
            copy.wait_send()

    up_products(0)
    forward(2)
    forward(1)
    up_products(1)
    up_products(2)
    add_on_way(1)
    add_on_way(2)
    hidden(1)
    hidden(0)
    hidden(2)
    loads[2].wait()
    swaps[2].wait_recv()
    down_products(1)
    down_products(0)
    down_products(2)

    for copy in swaps:
        copy.wait_send()
    near = [o for o, _, _ in CHUNKS[0]]
    unless_own([tok_copy(o, dx) for o in range(NY) for dx in range(NX if o in near else 1)])

    @pl.when(home)
    def _():
        for o in ORDER[len(near) :]:
            forward_copy(around(y, NY, o)).wait_send()

    for t in range(chunks):
        for j in range(NZ - 1):
            sum_copy(t, j).wait_send()
            hid_copy(t, j).wait_send()
    unless_own([out_copy(o, tile, n, dc) for o, tile, n in sorted(sum(CHUNKS, ())) for dc in range(NC)])

    total = jnp.zeros(recv_c.shape[1:], F32)
    for chunk in CHUNKS:
        for o, tile, n in chunk:
            for xx in range(NX):
                source = xx * NY + around(y, NY, NY - o)
                here = pl.ds(tile, n)
                pltpu.make_async_copy(
                    send_c.at[0, 0, here], recv_c.at[source, here], crs.at[source, tile]
                ).wait()
    for i in range(NG):
        total = total + recv_c[i].astype(F32)
    total = jnp.concatenate([total[:, :TILE], total[:, TILE:]], axis=2)
    out[...] = total.reshape(out.shape).astype(BF16)


def shards(tokens, gate_weight, up_weight, down_weight):
    rows, kd = tokens.shape
    ff, nd = down_weight.shape
    n, tiles, tall = len(CHUNKS), rows // TILE, NY * TILE
    dma = pltpu.SemaphoreType.DMA
    return pl.pallas_call(
        kernel,
        out_shape=pltpu.VMEM((rows, nd), BF16),
        in_specs=[pl.BlockSpec(memory_space=pl.ANY)] * 4,
        out_specs=pl.BlockSpec(memory_space=pltpu.VMEM),
        scratch_shapes=[
            pltpu.VMEM((rows, kd), BF16),
            pltpu.VMEM((NC * kd, ff), BF16),
            pltpu.VMEM((NC * kd, ff), BF16),
            pltpu.VMEM((NC, ff, nd), BF16),
            pltpu.VMEM((tiles, 2 * TILE, kd // 2), BF16),
            pltpu.VMEM((NY, NC, tiles, 2 * TILE, kd // 2), BF16),
            pltpu.VMEM((n, tall, ff), F32),
            pltpu.VMEM((n, tall, ff), F32),
            pltpu.VMEM((n, NZ - 1, 2 * TILE, ff), BF16),
            pltpu.VMEM((n, NZ - 1, 2 * TILE, ff), BF16),
            pltpu.VMEM((n, NZ, TILE, ff), BF16),
            pltpu.VMEM((NC, tall, nd), F32),
            pltpu.VMEM((NC, NY, tiles, 2 * TILE, nd // 2), BF16),
            pltpu.VMEM((NG, tiles, 2 * TILE, nd // 2), BF16),
            dma((4,)), dma((3,)), dma((3,)),
            dma((NX, NY)), dma((NY, NC)), dma((NY,)), dma((NY,)),
            dma((n, NZ - 1)), dma((n, NZ - 1)), dma((n, NZ - 1)), dma((n, NZ - 1)),
            dma((NC, NY, tiles)), dma((NG, tiles)),
        ],
        compiler_params=pltpu.CompilerParams(collective_id=0, has_side_effects=True, vmem_limit_bytes=60 << 20),
        name="feed_forward",
    )(tokens, gate_weight, up_weight, down_weight)


def solution(mesh):
    in_specs = (P(("depth", "row"), "col"), P("col", "row"), P("col", "row"), P("row", "col"))
    out_specs = P(("depth", "row"), "col")
    return jax.shard_map(shards, mesh=mesh, in_specs=in_specs, out_specs=out_specs, check_vma=False)
```
